256 devices in a mesh: row: 16 (over x_hi, y, core), col: 16 (over x_lo, z).
Axes of the slice: x: 4 (x_hi: 2, x_lo: 2; x = x_hi * 2 + x_lo), y: 4, z: 8, core: 2. Of those that a mesh axis runs over, the one named last changes fastest.
Arguments:
- activations: bfloat16 [1024, 8192], P('col', 'row'), may hold values from -6 to 6
- weight_gate: bfloat16 [8192, 14336], P('row', 'col'), may hold values from -0.0625 to 0.0625
- weight_up: bfloat16 [8192, 14336], P('row', 'col'), may hold values from -0.0625 to 0.0625
- weight_down: bfloat16 [14336, 8192], P('col', 'row'), may hold values from -0.046875 to 0.046875
- out_cotangent: bfloat16 [1024, 8192], P('col', 'row'), may hold values from -1.5 to 1.5
Outputs:
- block_out: bfloat16 [1024, 8192], P('col', 'row')
- input_gradient: bfloat16 [1024, 8192], P('col', 'row')
- gate_gradient: bfloat16 [8192, 14336], P('row', 'col')
- up_gradient: bfloat16 [8192, 14336], P('row', 'col')
- down_gradient: bfloat16 [14336, 8192], P('col', 'row')
The draws below stay inside these ranges and needn't reach their ends.
All inputs are finite; a program needn't handle non-finite values.
Results may differ from the reference program's by a relative error of at most 0.035.
Values may be sent and summed in bfloat16 or wider, within the bound.
No kernel may reach another device: no remote copies, remote signals or barrier semaphores. Data moves between devices by JAX's collectives and lax.ppermute only.
A program may use at most 64 MiB of HBM per device.

```python
import jax
import jax.numpy as jnp
from jax import lax

D = 8192
FF = 14336
TOKENS = 1024
N_ROW = 16
N_COL = 16


def raised(drawn, key, source, target, shards_of, factor):
    owner, partner = [(jnp.arange(drawn.shape[dim]) // (drawn.shape[dim] // shards_of)).reshape([-1 if axis == dim else 1 for axis in range(drawn.ndim)]) for dim in (source, target)]
    chosen = jax.random.permutation(key, shards_of)[partner]
    strong = (owner == chosen) | (owner == (partner + shards_of // 2) % shards_of)
    return jnp.where(strong, factor * drawn, drawn)


def levels(own_key, dims, cuts, smallest, largest):
    gain = 1.0
    for dim, shards_of in cuts:
        heights = jax.random.uniform(jax.random.fold_in(jax.random.fold_in(own_key, 6), dim), (shards_of,), jnp.float32, smallest / len(cuts), largest / len(cuts))
        gain = gain * jnp.repeat(jnp.exp(heights), dims[dim] // shards_of).reshape((-1,) + (1,) * (len(dims) - 1 - dim))
    return gain


def bell_draw(own_key, shape, deviation, reach, cuts=(), held_as=jnp.bfloat16):
    loudness = levels(own_key, shape, cuts, -0.22, 0.18) if cuts else 1.0
    entries = jax.random.normal(own_key, shape, jnp.float32) * deviation * loudness
    return jnp.minimum(jnp.maximum(entries, -reach), reach).astype(held_as)


def noise_with(rng, dims, scale, reach, cuts, heavy, kind=jnp.bfloat16):
    drawn = scale * jax.random.normal(rng, dims, jnp.float32)
    if cuts:
        drawn = drawn * levels(rng, dims, cuts, -0.22, 0.18)
    return jnp.clip(raised(drawn, jax.random.fold_in(rng, 3), *heavy), -reach, reach).astype(kind)


def setup_inputs(seed: int = 0) -> dict:
    key_list = jax.random.split(jax.random.key(seed), 6)
    activations = noise_with(key_list[0], (TOKENS, D), 1.0, 6.0, ((0, 16), (1, 16)), (1, 0, 16, 2.0))
    weight_gate = bell_draw(key_list[1], (D, FF), D ** -0.5, 0.0625, ((0, 16), (1, 16)))
    weight_up = bell_draw(key_list[2], (D, FF), D ** -0.5, 0.0625, ((0, 16), (1, 16)))
    weight_down = bell_draw(key_list[3], (FF, D), FF ** -0.5, 0.046875, ((0, 16), (1, 16)))
    out_cotangent = noise_with(key_list[4], (TOKENS, D), 0.25, 1.5, ((0, 16), (1, 16)), (1, 0, 16, 2.0))
    return dict(activations=activations, weight_gate=weight_gate, weight_up=weight_up, weight_down=weight_down, out_cotangent=out_cotangent)


def split_product(pairs, parts):
    width = pairs[0][0].shape[1] // parts
    rows = pairs[0][0].shape[0]
    cols = pairs[0][1].shape[1]

    def step(total, index):
        start = index * width
        term = jnp.zeros((rows, cols), jnp.float32)
        for left, right in pairs:
            left_block = lax.dynamic_slice_in_dim(left, start, width, 1)
            right_block = lax.dynamic_slice_in_dim(right, start, width, 0)
            term = term + jnp.dot(left_block, right_block, preferred_element_type=jnp.float32)
        rounded = lax.optimization_barrier(term.astype(jnp.bfloat16)).astype(jnp.float32)
        return total + rounded, None

    start_total = jnp.zeros((rows, cols), jnp.float32)
    total, unused = lax.scan(step, start_total, jnp.arange(parts, dtype=jnp.int32))
    return total


def swish_parts(gate):
    sigma = jax.nn.sigmoid(gate)
    return gate * sigma, sigma * (1.0 + gate * (1.0 - sigma))


def reference(activations, weight_gate, weight_up, weight_down, out_cotangent):
    gate = split_product([(activations, weight_gate)], N_ROW)
    up_value = split_product([(activations, weight_up)], N_ROW)
    swish, slope = swish_parts(gate)
    hidden = (swish * up_value).astype(jnp.bfloat16)
    block_out = split_product([(hidden, weight_down)], N_COL).astype(jnp.bfloat16)
    hidden_grad = split_product([(out_cotangent, weight_down.T)], N_ROW)
    gate_grad = (hidden_grad * up_value * slope).astype(jnp.bfloat16)
    up_grad = (hidden_grad * swish).astype(jnp.bfloat16)
    input_gradient = split_product([(gate_grad, weight_gate.T), (up_grad, weight_up.T)], N_COL).astype(jnp.bfloat16)
    gate_gradient = jnp.dot(activations.T, gate_grad, preferred_element_type=jnp.float32).astype(jnp.bfloat16)
    up_gradient = jnp.dot(activations.T, up_grad, preferred_element_type=jnp.float32).astype(jnp.bfloat16)
    down_gradient = jnp.dot(hidden.T, out_cotangent, preferred_element_type=jnp.float32).astype(jnp.bfloat16)
    return (block_out, input_gradient, gate_gradient, up_gradient, down_gradient)
```

```python
import jax
import jax.numpy as jnp
from jax import lax
from jax.sharding import PartitionSpec as P

BF16 = jnp.bfloat16
F32 = jnp.float32

SHIFTS = [(dx, dy) for dx in range(2) for dy in range(4)]


def row_index(x, y, core):
    return (x * 4 + y) * 2 + core


def to_core(value):
    return lax.ppermute(value, "row", [(i, i ^ 1) for i in range(16)])


def row_shift(value, dx, dy):
    pairs = [
        (row_index(x, y, core), row_index(x ^ dx, (y + dy) % 4, core))
        for x in range(2)
        for y in range(4)
        for core in range(2)
    ]
    return lax.ppermute(value, "row", pairs)


def z_shift(value, dz):
    pairs = [(x * 8 + z, x * 8 + (z + dz) % 8) for x in range(2) for z in range(8)]
    return lax.ppermute(value, "col", pairs)


def x_swap(value):
    return lax.ppermute(value, "col", [(j, j ^ 8) for j in range(16)])


def dot(left, right, left_dim, right_dim):
    return lax.dot_general(
        left, right, (((left_dim,), (right_dim,)), ((), ())), preferred_element_type=F32
    )


def swish_parts(gate):
    sigma = jax.nn.sigmoid(gate)
    return (gate * sigma, sigma * (1.0 + gate * (1.0 - sigma)))


def split_tokens(value, core):
    half = value.shape[0] // 2
    own = lax.dynamic_slice_in_dim(value, core * half, half, 0)
    other = lax.dynamic_slice_in_dim(value, (1 - core) * half, half, 0)
    return jnp.concatenate([own, to_core(other)], axis=1)


def gather_col(share, slots):
    pair = jnp.concatenate([share, x_swap(share)], axis=0)
    size = pair.shape[0]
    half = size // 2
    blocks = {0: pair}
    up = down = pair
    for step in range(1, 4):
        up, down = z_shift(up, 1), z_shift(down, -1)
        blocks[8 - step], blocks[step] = up, down
    blocks[4] = jnp.concatenate([z_shift(up[:half], 1), z_shift(down[half:], -1)], axis=0)
    total = jnp.zeros((8 * size, pair.shape[1]), pair.dtype)
    for k in range(8):
        total = lax.dynamic_update_slice_in_dim(total, blocks[k], slots[k] * size, 0)
    return total


def scatter_row(partial):
    size = partial.shape[0] // 8
    total = partial[:size].astype(F32)
    for n, (dx, dy) in enumerate(SHIFTS):
        if n:
            total = total + row_shift(partial[n * size : (n + 1) * size], dx, dy).astype(F32)
    return total


def gather_row(share):
    return jnp.concatenate(
        [row_shift(share, dx, -dy) if n else share for n, (dx, dy) in enumerate(SHIFTS)], axis=0
    )


def scatter_col(partial, slots, core):
    size = partial.shape[0] // 8
    half = size // 2

    def block(k):
        return lax.dynamic_slice_in_dim(partial, slots[k] * size, size, 0)

    def plus(left, right):
        return (left.astype(F32) + right.astype(F32)).astype(BF16)

    far = block(4)
    up, down = z_shift(far[:half], 1), z_shift(far[half:], -1)
    b_up, b_down = block(3), block(5)
    up = jnp.concatenate([plus(up, b_up[:half]), b_up[half:]], axis=0)
    down = jnp.concatenate([b_down[:half], plus(down, b_down[half:])], axis=0)
    for step in (2, 1):
        up = plus(z_shift(up, 1), block(step))
        down = plus(z_shift(down, -1), block(8 - step))
    total = block(0).astype(F32) + z_shift(up, 1).astype(F32) + z_shift(down, -1).astype(F32)
    total = (total[:half] + x_swap(total[half:].astype(BF16)).astype(F32)).astype(BF16)
    width = total.shape[1] // 2
    own, other = total[:, :width], to_core(total[:, width:])
    return jnp.where(
        core == 0,
        jnp.concatenate([own, other], axis=0),
        jnp.concatenate([other, own], axis=0),
    )


def per_device(activations, weight_gate, weight_up, weight_down, out_cotangent):
    row = lax.axis_index("row")
    core, chip = row % 2, row // 2
    x, y = chip // 4, chip % 4
    slots = [((k // 4) ^ x) * 4 + (k % 4 - y) % 4 for k in range(8)]
    width = weight_gate.shape[0]
    hidden_width = weight_gate.shape[1]

    acts = gather_col(split_tokens(activations, core), slots)
    cots = gather_col(split_tokens(out_cotangent, core), slots)
    both = jnp.concatenate([weight_gate, weight_up], axis=1)
    both = jnp.concatenate([both, to_core(both)], axis=0)
    down = jnp.concatenate([weight_down, to_core(weight_down)], axis=1)

    gate_up = scatter_row(dot(acts, both, 1, 0).astype(BF16))
    gate, up_value = gate_up[:, :hidden_width], gate_up[:, hidden_width:]
    hidden_grad = scatter_row(dot(cots, down, 1, 1).astype(BF16))
    swish, slope = swish_parts(gate)
    hidden = gather_row((swish * up_value).astype(BF16))
    block_out = scatter_col(dot(hidden, down, 1, 0).astype(BF16), slots, core)
    grads = gather_row(
        jnp.concatenate(
            [
                (hidden_grad * up_value * slope).astype(BF16),
                (hidden_grad * swish).astype(BF16),
            ],
            axis=1,
        )
    )
    input_gradient = scatter_col(dot(grads, both, 1, 1).astype(BF16), slots, core)

    down_other = to_core(dot(hidden, cots[:, width:], 0, 0).astype(BF16))
    down_gradient = (dot(hidden, cots[:, :width], 0, 0) + down_other.astype(F32)).astype(BF16)
    both_other = to_core(dot(acts[:, width:], grads, 0, 0).astype(BF16))
    both_gradient = (dot(acts[:, :width], grads, 0, 0) + both_other.astype(F32)).astype(BF16)
    return (
        block_out,
        input_gradient,
        both_gradient[:, :hidden_width],
        both_gradient[:, hidden_width:],
        down_gradient,
    )


def solution(mesh):
    return jax.shard_map(
        per_device,
        mesh=mesh,
        in_specs=(
            P("col", "row"),
            P("row", "col"),
            P("row", "col"),
            P("col", "row"),
            P("col", "row"),
        ),
        out_specs=(
            P("col", "row"),
            P("col", "row"),
            P("row", "col"),
            P("row", "col"),
            P("col", "row"),
        ),
        check_vma=False,
    )
```

```python
import jax
import jax.numpy as jnp
from jax import lax
from jax.experimental import pallas as pl
from jax.experimental.pallas import tpu as pltpu
from jax.sharding import PartitionSpec as P

BF16 = jnp.bfloat16
F32 = jnp.float32


def row_index(x, y, core):
    return (x * 4 + y) * 2 + core


def to_core(value):
    return lax.ppermute(value, "row", [(i, i ^ 1) for i in range(16)])


def row_shift(value, dx, dy):
    pairs = [
        (row_index(x, y, core), row_index(x ^ dx, (y + dy) % 4, core))
        for x in range(2)
        for y in range(4)
        for core in range(2)
    ]
    return lax.ppermute(value, "row", pairs)


def z_ring(value, ways, cores=(0, 1)):
    pairs = [
        (i * 16 + j, i * 16 + (j // 8) * 8 + (j % 8 + ways[i % 2]) % 8)
        for i in range(16)
        for j in range(16)
        if i % 2 in cores
    ]
    return lax.ppermute(value, ("row", "col"), pairs)


def home(value):
    pairs = [
        (i * 16 + j, (i ^ 1) * 16 + (j // 8) * 8 + (j % 8 + i % 2) % 8)
        for i in range(16)
        for j in range(16)
    ]
    return lax.ppermute(value, ("row", "col"), pairs)


def x_swap(value):
    return lax.ppermute(value, "col", [(j, j ^ 8) for j in range(16)])


def dot(left, right, left_dim, right_dim):
    return lax.dot_general(
        left, right, (((left_dim,), (right_dim,)), ((), ())), preferred_element_type=F32
    )


def swish_parts(gate):
    sigma = jax.nn.sigmoid(gate)
    return (gate * sigma, sigma * (1.0 + gate * (1.0 - sigma)))


def plus(left, right):
    return (left.astype(F32) + right.astype(F32)).astype(BF16)


def rows(parts):
    return jnp.concatenate(parts, axis=0)


def columns(parts):
    return jnp.concatenate(parts, axis=1)


def add_rows(value, start, more):
    stop = start + more.shape[0]
    parts = [value[:start], plus(value[start:stop], more), value[stop:]]
    return rows([part for part in parts if part.shape[0]])


def slot_numbers():
    row = lax.axis_index("row")
    core, y, x = row & 1, (row >> 1) & 3, row >> 3

    def both(slot):
        return [slot * 2 + (h ^ x) for h in range(2)]

    at_place = [both((p - y) & 3) for p in range(4)]
    of_block = [both((k - core - y) & 3) for k in range(4)]
    of_block.append(both(((3 - y) & 3) * core + 4 * (1 - core)))
    return core == 0, at_place, of_block


def gather_col(pair, numbers):
    size, width = pair.shape[0] // 2, pair.shape[1]
    total = jnp.zeros((10, size, width), BF16)
    block = pair
    for k in range(5):
        if k:
            block = z_ring(block, (1, -1), (0, 1) if k < 4 else (1,))
        halves = block.reshape(2, size, width)
        for h in range(2):
            total = lax.dynamic_update_slice(
                total, halves[h : h + 1], (numbers[k][h], 0, 0), allow_negative_indices=False
            )
    return total.reshape(10 * size, width)


def scatter_y_x(parts):
    own, first, up, down, last = parts
    size = up.shape[0]
    up, down = row_shift(up, 0, 1), row_shift(down, 0, -1)
    up = row_shift(add_rows(first, 0, up), 0, 1)
    down = row_shift(add_rows(last, size, down), 0, -1)
    total = own.astype(F32) + up.astype(F32) + down.astype(F32)
    return total[:size] + row_shift(total[size:].astype(BF16), 1, 0).astype(F32)


def scatter_x_y(near, far):
    size = near.shape[0] // 4
    half = size // 2
    near = plus(near, row_shift(far, 1, 0))
    up = row_shift(near[2 * size : 2 * size + half], 0, 1)
    down = row_shift(near[2 * size + half : 3 * size], 0, -1)
    up = row_shift(add_rows(near[size : 2 * size], 0, up), 0, 1)
    down = row_shift(add_rows(near[3 * size :], half, down), 0, -1)
    return near[:size].astype(F32) + up.astype(F32) + down.astype(F32)


def gather_x_y(share):
    size = share.shape[0]
    pair = rows([share, row_shift(share, 1, 0)])
    last, first = row_shift(pair, 0, 1), row_shift(pair, 0, -1)
    return [pair, first, row_shift(last[:size], 0, 1), row_shift(first[size:], 0, -1), last]


def gather_y_x(share):
    size = share.shape[0]
    half = size // 2
    last, first = row_shift(share, 0, 1), row_shift(share, 0, -1)
    near = rows([share, first, row_shift(last[:half], 0, 1), row_shift(first[half:], 0, -1), last])
    return near, row_shift(near, 1, 0)


def scatter_blocks(partial, numbers):
    size, width = partial.shape[0] // 8, partial.shape[1]
    slots = partial.reshape(8, size, width)
    return [
        rows(
            [
                lax.dynamic_slice(
                    slots, (number, 0, 0), (1, size, width), allow_negative_indices=False
                )
                for number in halves
            ]
        ).reshape(2 * size, width)
        for halves in numbers
    ]


def params(mib):
    return pltpu.CompilerParams(vmem_limit_bytes=mib * 2**20)


def whole_block(array):
    return pl.BlockSpec(array.shape, lambda step: (0, 0), pipeline_mode=pl.Buffered(1))


def forward_body(
    acts, cots, gate, gate_other, up, up_other, down, down_other, *outs
):
    *gate_ups, near, far = outs
    width, units = gate.shape
    acts, acts_other = acts[:, :width], acts[:, width:]
    cots, cots_other = cots[:, :width], cots[:, width:]

    def store(columns_of, own, other):
        term = (dot(acts, own[...], 1, 0) + dot(acts_other, other[...], 1, 0)).astype(BF16)

        def put(parts):
            start = 0
            for part in parts:
                stop = start + part.shape[0]
                part[:, columns_of] = term[start:stop]
                start = stop

        @pl.when(pl.program_id(0) == 0)
        def _():
            put(gate_ups[:2])

        @pl.when(pl.program_id(0) == 1)
        def _():
            put(gate_ups[2:])

    store(slice(0, units), gate, gate_other)
    store(slice(units, 2 * units), up, up_other)
    term = (dot(cots, down[...], 1, 1) + dot(cots_other, down_other[...], 1, 1)).astype(BF16)
    size = term.shape[0] // 4
    for n in range(2):
        near[n * size : (n + 1) * size, :] = term[2 * n * size : (2 * n + 1) * size]
        far[n * size : (n + 1) * size, :] = term[(2 * n + 1) * size : (2 * n + 2) * size]


def forward(acts, cots, weights):
    units = weights[0].shape[1]
    size = acts.shape[0] // 10
    pieces = [(n * size, 2 * units) for n in (2, 2, 1, 1, 2)]
    halves = [(4 * size, units)] * 2
    outs = pl.pallas_call(
        forward_body,
        grid=(2,),
        in_specs=[pl.BlockSpec((4 * size, acts.shape[1]), lambda n: (n, 0))] * 2
        + [whole_block(weight) for weight in weights],
        out_specs=[pl.BlockSpec(shape, lambda n: (0, 0)) for shape in pieces]
        + [pl.BlockSpec((shape[0] // 2, shape[1]), lambda n: (n, 0)) for shape in halves],
        out_shape=[jax.ShapeDtypeStruct(shape, BF16) for shape in pieces + halves],
        compiler_params=params(24),
    )(acts, cots, *weights)
    return outs[:5], outs[5:]


def backward_body(
    near, far, g0, g1, g2, g3, g4, gate, gate_other, up, up_other, down, down_other,
    out, inner, hidden, gate_grad, up_grad,
):
    units = hidden.shape[1]
    width = gate.shape[0]
    size = near.shape[0] // 2
    for n in range(2):
        hidden[2 * n * size : (2 * n + 1) * size, :] = near[n * size : (n + 1) * size, :]
        hidden[(2 * n + 1) * size : (2 * n + 2) * size, :] = far[n * size : (n + 1) * size, :]

    def assemble(parts):
        start = 0
        for part in parts:
            stop = start + part.shape[0]
            gate_grad[start:stop, :] = part[:, :units]
            up_grad[start:stop, :] = part[:, units:]
            start = stop

    @pl.when(pl.program_id(0) == 0)
    def _():
        assemble((g0, g1))

    @pl.when(pl.program_id(0) == 1)
    def _():
        assemble((g2, g3, g4))

    for n, (g, u, d) in enumerate(((gate, up, down), (gate_other, up_other, down_other))):
        columns_of = slice(n * width, (n + 1) * width)
        out[:, columns_of] = dot(hidden[...], d[...], 1, 0).astype(BF16)
        inner[:, columns_of] = (
            dot(gate_grad[...], g[...], 1, 1) + dot(up_grad[...], u[...], 1, 1)
        ).astype(BF16)


def backward(near, far, grads, weights):
    width, units = weights[0].shape
    tokens = 2 * near.shape[0]
    shapes = [(tokens, 2 * width)] * 2 + [(tokens, units)] * 3
    halved = lambda shape: pl.BlockSpec((shape[0] // 2, shape[1]), lambda n: (n, 0))
    return pl.pallas_call(
        backward_body,
        grid=(2,),
        in_specs=[halved(near.shape), halved(far.shape)]
        + [whole_block(array) for array in (*grads, *weights)],
        out_specs=[halved(shape) for shape in shapes],
        out_shape=[jax.ShapeDtypeStruct(shape, BF16) for shape in shapes],
        compiler_params=params(24),
    )(near, far, *grads, *weights)


def assemble_body(acts, cots, near, own_far, near_far, acts_out, cots_out):
    tokens, width = acts.shape
    for n, (own, out) in enumerate(((acts, acts_out), (cots, cots_out))):
        part = slice(n * tokens, (n + 1) * tokens)
        out[:tokens, :width] = own[...]
        out[tokens:, :width] = near[part, :]
        out[:tokens, width:] = own_far[part, :]
        out[tokens:, width:] = near_far[part, :]


def assemble(acts, cots, near, own_far, near_far):
    tokens, width = acts.shape
    shape = jax.ShapeDtypeStruct((2 * tokens, 2 * width), BF16)
    return pl.pallas_call(assemble_body, out_shape=[shape, shape], compiler_params=params(8))(
        acts, cots, near, own_far, near_far
    )


def per_device(activations, weight_gate, weight_up, weight_down, out_cotangent):
    width, units = weight_gate.shape
    tokens = activations.shape[0]
    (first_core, at_place, of_block), activations, out_cotangent = lax.optimization_barrier(
        (slot_numbers(), activations, out_cotangent)
    )

    mine = rows([activations, out_cotangent])
    near = x_swap(mine)
    acts, cots = assemble(activations, out_cotangent, near, to_core(mine), to_core(near))
    weights = [
        part for weight in (weight_gate, weight_up, weight_down) for part in (weight, to_core(weight))
    ]
    acts, cots = gather_col(acts, of_block), gather_col(cots, of_block)

    gate_ups, halves = forward(acts, cots, weights)
    hidden_grad, gate_up = scatter_x_y(*halves), scatter_y_x(gate_ups)
    gate, up_value = gate_up[:, :units], gate_up[:, units:]
    swish, slope = swish_parts(gate)
    hidden_share, grad_share = lax.optimization_barrier(
        (
            (swish * up_value).astype(BF16),
            columns(
                [
                    (hidden_grad * up_value * slope).astype(BF16),
                    (hidden_grad * swish).astype(BF16),
                ]
            ),
        )
    )
    grads, (near, far) = gather_x_y(grad_share), gather_y_x(hidden_share)
    block_out, input_gradient, hidden, gate_grad, up_grad = backward(near, far, grads, weights)

    def summed(own, other):
        return (own + to_core(other.astype(BF16)).astype(F32)).astype(BF16)

    outs, ins = scatter_blocks(block_out, at_place), scatter_blocks(input_gradient, at_place)
    ways = (-1, 1)
    out, inner = z_ring(outs[3], ways), z_ring(ins[3], ways)
    (h, g, u), out = lax.optimization_barrier(((hidden, gate_grad, up_grad), out))
    a_own, a_other = acts[: 8 * tokens, :width], acts[: 8 * tokens, width:]
    c_own, c_other = cots[: 8 * tokens, :width], cots[: 8 * tokens, width:]
    gate_gradient = summed(dot(a_own, g, 0, 0), dot(a_other, g, 0, 0))
    up_gradient = summed(dot(a_own, u, 0, 0), dot(a_other, u, 0, 0))
    down_gradient = summed(dot(h, c_own, 0, 0), dot(h, c_other, 0, 0))
    for j in (2, 1):
        out, inner = z_ring(plus(outs[j], out), ways), z_ring(plus(ins[j], inner), ways)
    total = rows([plus(outs[0], out), plus(ins[0], inner)])
    crossed, moved = home(total[:, width:]), z_ring(total[:, :width], (-1, 1), (1,))
    total = plus(jnp.where(first_core, total[:, :width], moved), crossed)
    total, gate_gradient, up_gradient = lax.optimization_barrier(
        (total, gate_gradient, up_gradient)
    )
    mine = [total[n * tokens : (n + 1) * tokens] for n in range(4)]
    other = x_swap(rows([mine[1], mine[3]]))
    other, down_gradient = lax.optimization_barrier((other, down_gradient))
    return (
        plus(mine[0], other[:tokens]),
        plus(mine[2], other[tokens:]),
        gate_gradient,
        up_gradient,
        down_gradient,
    )


def solution(mesh):
    return jax.shard_map(
        per_device,
        mesh=mesh,
        in_specs=(
            P("col", "row"),
            P("row", "col"),
            P("row", "col"),
            P("col", "row"),
            P("col", "row"),
        ),
        out_specs=(
            P("col", "row"),
            P("col", "row"),
            P("row", "col"),
            P("row", "col"),
            P("col", "row"),
        ),
        check_vma=False,
    )
```

```python
import jax
import jax.numpy as jnp
from jax import lax
from jax.experimental import pallas as pl
from jax.experimental.pallas import tpu as pltpu
from jax.sharding import PartitionSpec as P

BF16 = jnp.bfloat16
F32 = jnp.float32


def row_index(x, y, core):
    return (x * 4 + y) * 2 + core


def to_core(value):
    return lax.ppermute(value, "row", [(i, i ^ 1) for i in range(16)])


def row_shift(value, dx, dy):
    pairs = [
        (row_index(x, y, core), row_index(x ^ dx, (y + dy) % 4, core))
        for x in range(2)
        for y in range(4)
        for core in range(2)
    ]
    return lax.ppermute(value, "row", pairs)


def z_ring(value, ways):
    pairs = [
        (i * 16 + j, i * 16 + (j // 8) * 8 + (j % 8 + ways[i % 2]) % 8)
        for i in range(16)
        for j in range(16)
    ]
    return lax.ppermute(value, ("row", "col"), pairs)


def x_swap(value):
    return lax.ppermute(value, "col", [(j, j ^ 8) for j in range(16)])


def dot(left, right, left_dim, right_dim):
    return lax.dot_general(
        left, right, (((left_dim,), (right_dim,)), ((), ())), preferred_element_type=F32
    )


def swish_parts(gate):
    sigma = jax.nn.sigmoid(gate)
    return (gate * sigma, sigma * (1.0 + gate * (1.0 - sigma)))


def plus(left, right):
    return (left.astype(F32) + right.astype(F32)).astype(BF16)


def rows(parts):
    return jnp.concatenate(parts, axis=0)


def columns(parts):
    return jnp.concatenate(parts, axis=1)


def add_rows(value, start, more):
    stop = start + more.shape[0]
    parts = [value[:start], plus(value[start:stop], more), value[stop:]]
    return rows([part for part in parts if part.shape[0]])


def slot_numbers():
    row = lax.axis_index("row")
    core, y, x = row & 1, (row >> 1) & 3, row >> 3
    return core, core == 0, [(((p >> 1) - y) & 3) * 2 + ((p & 1) ^ x) for p in range(8)]


def unit_of(pair, which):
    size, width = pair.shape[0] // 2, pair.shape[1]
    return lax.dynamic_slice(
        pair.reshape(2, size, width), (which, 0, 0), (1, size, width), allow_negative_indices=False
    ).reshape(size, width)


def gather_col(pair, core, slots):
    size, width = pair.shape[0] // 2, pair.shape[1]
    units, block = [unit_of(pair, core)], pair
    for _ in range(3):
        block = z_ring(block, (1, -1))
        units += [block[:size], block[size:]]
    units.append(z_ring(unit_of(block, core), (1, -1)))
    total = jnp.zeros((8, size, width), BF16)
    for unit, slot in zip(units, slots):
        total = lax.dynamic_update_slice(
            total, unit.reshape(1, size, width), (slot, 0, 0), allow_negative_indices=False
        )
    return total.reshape(8 * size, width)


def scatter_y_x(parts):
    own, first, up, down, last = parts
    size = up.shape[0]
    up, down = row_shift(up, 0, 1), row_shift(down, 0, -1)
    up = row_shift(add_rows(first, 0, up), 0, 1)
    down = row_shift(add_rows(last, size, down), 0, -1)
    total = own.astype(F32) + up.astype(F32) + down.astype(F32)
    return total[:size] + row_shift(total[size:].astype(BF16), 1, 0).astype(F32)


def scatter_x_y(near, far):
    size = near.shape[0] // 4
    near = plus(near, row_shift(far, 1, 0))
    total = near[:size].astype(F32)
    for dy in (2, 1, 3):
        total = total + row_shift(near[dy * size : (dy + 1) * size], 0, dy).astype(F32)
    return total


def gather_row(share, other):
    size = share.shape[0]
    pair = rows([share, row_shift(share, 1, 0)])
    near = [other] + [row_shift(other, 0, -dy) for dy in (1, 2, 3)]
    last, first = row_shift(pair, 0, 1), row_shift(pair, 0, -1)
    near = rows(near)
    far = row_shift(near, 1, 0)
    up, down = row_shift(last[:size], 0, 1), row_shift(first[size:], 0, -1)
    return (pair, first, up, down, last), (near, far)


def scatter_units(partial, slots):
    size, width = partial.shape[0] // 8, partial.shape[1]
    return [
        lax.dynamic_slice(
            partial.reshape(8, size, width), (slot, 0, 0), (1, size, width), allow_negative_indices=False
        ).reshape(size, width)
        for slot in slots
    ]


def one_unit(unit, first):
    none = jnp.zeros_like(unit)
    return rows([jnp.where(first, unit, none), jnp.where(first, none, unit)])


def params(mib):
    return pltpu.CompilerParams(vmem_limit_bytes=mib * 2**20)


def whole_block(array):
    return pl.BlockSpec(array.shape, lambda step: (0, 0), pipeline_mode=pl.Buffered(1))


def gate_up_body(acts, gate, gate_other, up, up_other, *parts):
    width, units = gate.shape
    acts, acts_other = acts[:, :width], acts[:, width:]

    def store(columns_of, own, other):
        term = (dot(acts, own[...], 1, 0) + dot(acts_other, other[...], 1, 0)).astype(BF16)

        def put(parts):
            start = 0
            for part in parts:
                stop = start + part.shape[0]
                part[:, columns_of] = term[start:stop]
                start = stop

        @pl.when(pl.program_id(0) == 0)
        def _():
            put(parts[:2])

        @pl.when(pl.program_id(0) == 1)
        def _():
            put(parts[2:])

    store(slice(0, units), gate, gate_other)
    store(slice(units, 2 * units), up, up_other)


def gate_up_product(acts, weights):
    units = weights[0].shape[1]
    size = acts.shape[0] // 8
    shapes = [(n * size, 2 * units) for n in (2, 2, 1, 1, 2)]
    return pl.pallas_call(
        gate_up_body,
        grid=(2,),
        in_specs=[pl.BlockSpec((4 * size, acts.shape[1]), lambda n: (n, 0))]
        + [whole_block(weight) for weight in weights],
        out_specs=[pl.BlockSpec(shape, lambda n: (0, 0)) for shape in shapes],
        out_shape=[jax.ShapeDtypeStruct(shape, BF16) for shape in shapes],
        compiler_params=params(20),
    )(acts, *weights)


def hidden_grad_body(cots, down, down_other, near, far):
    width = down.shape[1]
    term = dot(cots[:, :width], down[...], 1, 1) + dot(cots[:, width:], down_other[...], 1, 1)
    term = term.astype(BF16)
    size = term.shape[0] // 4
    for n in range(2):
        near[n * size : (n + 1) * size, :] = term[2 * n * size : (2 * n + 1) * size]
        far[n * size : (n + 1) * size, :] = term[(2 * n + 1) * size : (2 * n + 2) * size]


def hidden_grad_product(cots, weights):
    units = weights[0].shape[0]
    size = cots.shape[0] // 8
    return pl.pallas_call(
        hidden_grad_body,
        grid=(2,),
        in_specs=[pl.BlockSpec((4 * size, cots.shape[1]), lambda n: (n, 0))]
        + [whole_block(weight) for weight in weights],
        out_specs=[pl.BlockSpec((2 * size, units), lambda n: (n, 0))] * 2,
        out_shape=[jax.ShapeDtypeStruct((4 * size, units), BF16)] * 2,
        compiler_params=params(16),
    )(cots, *weights)


def out_body(near, far, down, down_other, out, hidden):
    size = near.shape[0] // 2
    width = down.shape[1]
    for n in range(2):
        hidden[2 * n * size : (2 * n + 1) * size, :] = near[n * size : (n + 1) * size, :]
        hidden[(2 * n + 1) * size : (2 * n + 2) * size, :] = far[n * size : (n + 1) * size, :]
    out[:, :width] = dot(hidden[...], down[...], 1, 0).astype(BF16)
    out[:, width:] = dot(hidden[...], down_other[...], 1, 0).astype(BF16)


def halved(shape):
    return pl.BlockSpec((shape[0] // 2, shape[1]), lambda n: (n, 0))


def out_product(near, far, weights):
    units, width = weights[0].shape
    tokens = 2 * near.shape[0]
    shapes = [(tokens, 2 * width), (tokens, units)]
    return pl.pallas_call(
        out_body,
        grid=(2,),
        in_specs=[halved(near.shape)] * 2 + [whole_block(weight) for weight in weights],
        out_specs=[halved(shape) for shape in shapes],
        out_shape=[jax.ShapeDtypeStruct(shape, BF16) for shape in shapes],
        compiler_params=params(16),
    )(near, far, *weights)


def inner_body(
    g0, g1, g2, g3, g4, gate, gate_other, up, up_other, inner, gate_grad, up_grad
):
    width, units = gate.shape

    def assemble(parts):
        start = 0
        for part in parts:
            stop = start + part.shape[0]
            gate_grad[start:stop, :] = part[:, :units]
            up_grad[start:stop, :] = part[:, units:]
            start = stop

    @pl.when(pl.program_id(0) == 0)
    def _():
        assemble((g0, g1))

    @pl.when(pl.program_id(0) == 1)
    def _():
        assemble((g2, g3, g4))

    for n, (g, u) in enumerate(((gate, up), (gate_other, up_other))):
        inner[:, n * width : (n + 1) * width] = (
            dot(gate_grad[...], g[...], 1, 1) + dot(up_grad[...], u[...], 1, 1)
        ).astype(BF16)


def inner_product(grads, weights):
    width, units = weights[0].shape
    tokens = sum(part.shape[0] for part in grads)
    shapes = [(tokens, 2 * width)] + [(tokens, units)] * 2
    return pl.pallas_call(
        inner_body,
        grid=(2,),
        in_specs=[whole_block(array) for array in (*grads, *weights)],
        out_specs=[halved(shape) for shape in shapes],
        out_shape=[jax.ShapeDtypeStruct(shape, BF16) for shape in shapes],
        compiler_params=params(20),
    )(*grads, *weights)


def beside_body(own, other, pair):
    width = own.shape[1]
    pair[:, :width] = own[...]
    pair[:, width:] = other[...]


def with_partners(value):
    own = rows([value, x_swap(value)])
    return pl.pallas_call(
        beside_body,
        out_shape=jax.ShapeDtypeStruct((own.shape[0], 2 * own.shape[1]), BF16),
        compiler_params=params(8),
    )(own, to_core(own))


def per_device(activations, weight_gate, weight_up, weight_down, out_cotangent):
    width, units = weight_gate.shape
    tokens = activations.shape[0]
    (core, first, slots), activations, out_cotangent = lax.optimization_barrier(
        (slot_numbers(), activations, out_cotangent)
    )

    acts, cots = with_partners(activations), with_partners(out_cotangent)
    weights = (weight_gate, weight_up, weight_down)
    gate_weights, up_weights, down_weights = ((w, to_core(w)) for w in weights)
    acts, cots = gather_col(acts, core, slots), gather_col(cots, core, slots)
    hidden_grad = scatter_x_y(*hidden_grad_product(cots, down_weights))
    gate_up = scatter_y_x(gate_up_product(acts, (*gate_weights, *up_weights)))
    gate, up_value = gate_up[:, :units], gate_up[:, units:]
    swish, slope = swish_parts(gate)
    hidden_share, grad_share = lax.optimization_barrier(
        (
            (swish * up_value).astype(BF16),
            columns(
                [
                    (hidden_grad * up_value * slope).astype(BF16),
                    (hidden_grad * swish).astype(BF16),
                ]
            ),
        )
    )
    grads, (near, far) = gather_row(grad_share, hidden_share)
    block_out, hidden = out_product(near, far, down_weights)
    input_gradient, gate_grad, up_grad = inner_product(grads, (*gate_weights, *up_weights))

    def summed(own, other):
        return (own + to_core(other.astype(BF16)).astype(F32)).astype(BF16)

    partials = [scatter_units(partial, slots) for partial in (block_out, input_gradient)]
    sums = [z_ring(units[7], (-1, 1)) for units in partials]
    (h, g, u), sums[1] = lax.optimization_barrier(((hidden, gate_grad, up_grad), sums[1]))
    gate_gradient = summed(dot(acts[:, :width], g, 0, 0), dot(acts[:, width:], g, 0, 0))
    up_gradient = summed(dot(acts[:, :width], u, 0, 0), dot(acts[:, width:], u, 0, 0))
    down_gradient = summed(dot(h, cots[:, :width], 0, 0), dot(h, cots[:, width:], 0, 0))
    sums = [one_unit(total, first) for total in sums]
    for p in (5, 3, 1):
        sums = [
            z_ring(plus(rows(units[p : p + 2]), total), (-1, 1))
            for units, total in zip(partials, sums)
        ]
    total = rows(
        [plus(one_unit(units[0], first), total) for units, total in zip(partials, sums)]
    )
    total = plus(total[:, :width], to_core(total[:, width:]))
    mine = [total[n * tokens : (n + 1) * tokens] for n in range(4)]
    other, gate_gradient, up_gradient, down_gradient = lax.optimization_barrier(
        (x_swap(rows([mine[1], mine[3]])), gate_gradient, up_gradient, down_gradient)
    )
    return (
        plus(mine[0], other[:tokens]),
        plus(mine[2], other[tokens:]),
        gate_gradient,
        up_gradient,
        down_gradient,
    )


def solution(mesh):
    return jax.shard_map(
        per_device,
        mesh=mesh,
        in_specs=(
            P("col", "row"),
            P("row", "col"),
            P("row", "col"),
            P("col", "row"),
            P("col", "row"),
        ),
        out_specs=(
            P("col", "row"),
            P("col", "row"),
            P("row", "col"),
            P("row", "col"),
            P("col", "row"),
        ),
        check_vma=False,
    )
```

```python
import jax
import jax.numpy as jnp
from jax import lax
from jax.experimental import pallas as pl
from jax.experimental.pallas import tpu as pltpu
from jax.sharding import PartitionSpec as P

BF16 = jnp.bfloat16
F32 = jnp.float32


def row_index(x, y, core):
    return (x * 4 + y) * 2 + core


def to_core(value):
    return lax.ppermute(value, "row", [(i, i ^ 1) for i in range(16)])


def row_shift(value, dx, dy):
    pairs = [
        (row_index(x, y, core), row_index(x ^ dx, (y + dy) % 4, core))
        for x in range(2)
        for y in range(4)
        for core in range(2)
    ]
    return lax.ppermute(value, "row", pairs)


def z_ring(value, ways):
    pairs = [
        (i * 16 + j, i * 16 + (j // 8) * 8 + (j % 8 + ways[i % 2]) % 8)
        for i in range(16)
        for j in range(16)
    ]
    return lax.ppermute(value, ("row", "col"), pairs)


def x_swap(value):
    return lax.ppermute(value, "col", [(j, j ^ 8) for j in range(16)])


def dot(left, right, left_dim, right_dim):
    return lax.dot_general(
        left, right, (((left_dim,), (right_dim,)), ((), ())), preferred_element_type=F32
    )


def swish_parts(gate):
    sigma = jax.nn.sigmoid(gate)
    return (gate * sigma, sigma * (1.0 + gate * (1.0 - sigma)))


def plus(left, right):
    return (left.astype(F32) + right.astype(F32)).astype(BF16)


def rows(parts):
    return jnp.concatenate(parts, axis=0)


def columns(parts):
    return jnp.concatenate(parts, axis=1)


def add_rows(value, start, more):
    stop = start + more.shape[0]
    parts = [value[:start], plus(value[start:stop], more), value[stop:]]
    return rows([part for part in parts if part.shape[0]])


def slot_numbers():
    row = lax.axis_index("row")
    core, y, x = row & 1, (row >> 1) & 3, row >> 3
    return core, core == 0, [(((p >> 1) - y) & 3) * 2 + ((p & 1) ^ x) for p in range(8)]


def unit_of(pair, which):
    size, width = pair.shape[0] // 2, pair.shape[1]
    return lax.dynamic_slice(
        pair.reshape(2, size, width), (which, 0, 0), (1, size, width), allow_negative_indices=False
    ).reshape(size, width)


def gather_col(pair, core, slots):
    size, width = pair.shape[0] // 2, pair.shape[1]
    units, block = [unit_of(pair, core)], pair
    for _ in range(3):
        block = z_ring(block, (1, -1))
        units += [block[:size], block[size:]]
    units.append(z_ring(unit_of(block, core), (1, -1)))
    total = jnp.zeros((8, size, width), BF16)
    for unit, slot in zip(units, slots):
        total = lax.dynamic_update_slice(
            total, unit.reshape(1, size, width), (slot, 0, 0), allow_negative_indices=False
        )
    return total.reshape(8 * size, width)


def scatter_y_x(parts):
    own, first, up, down, last = parts
    size = up.shape[0]
    up, down = row_shift(up, 0, 1), row_shift(down, 0, -1)
    up = row_shift(add_rows(first, 0, up), 0, 1)
    down = row_shift(add_rows(last, size, down), 0, -1)
    total = own.astype(F32) + up.astype(F32) + down.astype(F32)
    return total[:size] + row_shift(total[size:].astype(BF16), 1, 0).astype(F32)


def scatter_x_y(near, far):
    size = near.shape[0] // 4
    near = plus(near, row_shift(far, 1, 0))
    total = near[:size].astype(F32)
    for dy in (2, 1, 3):
        total = total + row_shift(near[dy * size : (dy + 1) * size], 0, dy).astype(F32)
    return total


def gather_row(share, other):
    size = share.shape[0]
    pair = rows([share, row_shift(share, 1, 0)])
    near = [other] + [row_shift(other, 0, -dy) for dy in (1, 2, 3)]
    last, first = row_shift(pair, 0, 1), row_shift(pair, 0, -1)
    near = rows(near)
    far = row_shift(near, 1, 0)
    up, down = row_shift(last[:size], 0, 1), row_shift(first[size:], 0, -1)
    return (pair, first, up, down, last), (near, far)


def scatter_units(partial, slots):
    size, width = partial.shape[0] // 8, partial.shape[1]
    return [
        lax.dynamic_slice(
            partial.reshape(8, size, width), (slot, 0, 0), (1, size, width), allow_negative_indices=False
        ).reshape(size, width)
        for slot in slots
    ]


def one_unit(unit, first):
    none = jnp.zeros_like(unit)
    return rows([jnp.where(first, unit, none), jnp.where(first, none, unit)])


def params(mib):
    return pltpu.CompilerParams(vmem_limit_bytes=mib * 2**20)


def whole_block(array):
    return pl.BlockSpec(array.shape, lambda step: (0, 0), pipeline_mode=pl.Buffered(1))


def gate_up_body(acts, gate, gate_other, up, up_other, *parts):
    width, units = gate.shape
    acts, acts_other = acts[:, :width], acts[:, width:]

    def store(columns_of, own, other):
        term = (dot(acts, own[...], 1, 0) + dot(acts_other, other[...], 1, 0)).astype(BF16)

        def put(parts):
            start = 0
            for part in parts:
                stop = start + part.shape[0]
                part[:, columns_of] = term[start:stop]
                start = stop

        @pl.when(pl.program_id(0) == 0)
        def _():
            put(parts[:2])

        @pl.when(pl.program_id(0) == 1)
        def _():
            put(parts[2:])

    store(slice(0, units), gate, gate_other)
    store(slice(units, 2 * units), up, up_other)


def gate_up_product(acts, weights):
    units = weights[0].shape[1]
    size = acts.shape[0] // 8
    shapes = [(n * size, 2 * units) for n in (2, 2, 1, 1, 2)]
    return pl.pallas_call(
        gate_up_body,
        grid=(2,),
        in_specs=[pl.BlockSpec((4 * size, acts.shape[1]), lambda n: (n, 0))]
        + [whole_block(weight) for weight in weights],
        out_specs=[pl.BlockSpec(shape, lambda n: (0, 0)) for shape in shapes],
        out_shape=[jax.ShapeDtypeStruct(shape, BF16) for shape in shapes],
        compiler_params=params(20),
    )(acts, *weights)


def hidden_grad_body(cots, down, down_other, near, far):
    width = down.shape[1]
    term = dot(cots[:, :width], down[...], 1, 1) + dot(cots[:, width:], down_other[...], 1, 1)
    term = term.astype(BF16)
    size = term.shape[0] // 4
    for n in range(2):
        near[n * size : (n + 1) * size, :] = term[2 * n * size : (2 * n + 1) * size]
        far[n * size : (n + 1) * size, :] = term[(2 * n + 1) * size : (2 * n + 2) * size]


def hidden_grad_product(cots, weights):
    units = weights[0].shape[0]
    size = cots.shape[0] // 8
    return pl.pallas_call(
        hidden_grad_body,
        grid=(2,),
        in_specs=[pl.BlockSpec((4 * size, cots.shape[1]), lambda n: (n, 0))]
        + [whole_block(weight) for weight in weights],
        out_specs=[pl.BlockSpec((2 * size, units), lambda n: (n, 0))] * 2,
        out_shape=[jax.ShapeDtypeStruct((4 * size, units), BF16)] * 2,
        compiler_params=params(16),
    )(cots, *weights)


def out_body(near, far, down, down_other, out, hidden):
    size = near.shape[0] // 2
    width = down.shape[1]
    for n in range(2):
        hidden[2 * n * size : (2 * n + 1) * size, :] = near[n * size : (n + 1) * size, :]
        hidden[(2 * n + 1) * size : (2 * n + 2) * size, :] = far[n * size : (n + 1) * size, :]
    out[:, :width] = dot(hidden[...], down[...], 1, 0).astype(BF16)
    out[:, width:] = dot(hidden[...], down_other[...], 1, 0).astype(BF16)


def halved(shape):
    return pl.BlockSpec((shape[0] // 2, shape[1]), lambda n: (n, 0))


def out_product(near, far, weights):
    units, width = weights[0].shape
    tokens = 2 * near.shape[0]
    shapes = [(tokens, 2 * width), (tokens, units)]
    return pl.pallas_call(
        out_body,
        grid=(2,),
        in_specs=[halved(near.shape)] * 2 + [whole_block(weight) for weight in weights],
        out_specs=[halved(shape) for shape in shapes],
        out_shape=[jax.ShapeDtypeStruct(shape, BF16) for shape in shapes],
        compiler_params=params(16),
    )(near, far, *weights)


def inner_body(
    g0, g1, g2, g3, g4, gate, gate_other, up, up_other, inner, gate_grad, up_grad
):
    width, units = gate.shape

    def assemble(parts):
        start = 0
        for part in parts:
            stop = start + part.shape[0]
            gate_grad[start:stop, :] = part[:, :units]
            up_grad[start:stop, :] = part[:, units:]
            start = stop

    @pl.when(pl.program_id(0) == 0)
    def _():
        assemble((g0, g1))

    @pl.when(pl.program_id(0) == 1)
    def _():
        assemble((g2, g3, g4))

    for n, (g, u) in enumerate(((gate, up), (gate_other, up_other))):
        inner[:, n * width : (n + 1) * width] = (
            dot(gate_grad[...], g[...], 1, 1) + dot(up_grad[...], u[...], 1, 1)
        ).astype(BF16)


def inner_product(grads, weights):
    width, units = weights[0].shape
    tokens = sum(part.shape[0] for part in grads)
    shapes = [(tokens, 2 * width)] + [(tokens, units)] * 2
    return pl.pallas_call(
        inner_body,
        grid=(2,),
        in_specs=[whole_block(array) for array in (*grads, *weights)],
        out_specs=[halved(shape) for shape in shapes],
        out_shape=[jax.ShapeDtypeStruct(shape, BF16) for shape in shapes],
        compiler_params=params(20),
    )(*grads, *weights)


def beside_body(own, other, pair):
    width = own.shape[1]
    pair[:, :width] = own[...]
    pair[:, width:] = other[...]


def with_partners(value):
    own = rows([value, x_swap(value)])
    return pl.pallas_call(
        beside_body,
        out_shape=jax.ShapeDtypeStruct((own.shape[0], 2 * own.shape[1]), BF16),
        compiler_params=params(8),
    )(own, to_core(own))


def per_device(activations, weight_gate, weight_up, weight_down, out_cotangent):
    width, units = weight_gate.shape
    tokens = activations.shape[0]
    (core, first, slots), activations, out_cotangent = lax.optimization_barrier(
        (slot_numbers(), activations, out_cotangent)
    )

    acts, cots = with_partners(activations), with_partners(out_cotangent)
    weights = (weight_gate, weight_up, weight_down)
    gate_weights, up_weights, down_weights = ((w, to_core(w)) for w in weights)
    acts, cots = gather_col(acts, core, slots), gather_col(cots, core, slots)
    hidden_grad = scatter_x_y(*hidden_grad_product(cots, down_weights))
    gate_up = scatter_y_x(gate_up_product(acts, (*gate_weights, *up_weights)))
    gate, up_value = gate_up[:, :units], gate_up[:, units:]
    swish, slope = swish_parts(gate)
    hidden_share, grad_share = lax.optimization_barrier(
        (
            (swish * up_value).astype(BF16),
            columns(
                [
                    (hidden_grad * up_value * slope).astype(BF16),
                    (hidden_grad * swish).astype(BF16),
                ]
            ),
        )
    )
    grads, (near, far) = gather_row(grad_share, hidden_share)
    block_out, hidden = out_product(near, far, down_weights)
    input_gradient, gate_grad, up_grad = inner_product(grads, (*gate_weights, *up_weights))

    partials = [scatter_units(partial, slots) for partial in (block_out, input_gradient)]
    sums = [z_ring(units[7], (-1, 1)) for units in partials]
    (h, g, u), sums[1] = lax.optimization_barrier(((hidden, gate_grad, up_grad), sums[1]))
    sent = [
        to_core(dot(left, right, 0, 0).astype(BF16))
        for left, right in ((acts[:, width:], g), (acts[:, width:], u), (h, cots[:, width:]))
    ]
    sums = [one_unit(total, first) for total in sums]
    for p in (5, 3, 1):
        sums = [
            z_ring(plus(rows(units[p : p + 2]), total), (-1, 1))
            for units, total in zip(partials, sums)
        ]
    total = rows(
        [plus(one_unit(units[0], first), total) for units, total in zip(partials, sums)]
    )
    total = plus(total[:, :width], to_core(total[:, width:]))
    total, sent = lax.optimization_barrier((total, sent))
    mine = [total[n * tokens : (n + 1) * tokens] for n in range(4)]
    other = x_swap(rows([mine[1], mine[3]]))
    gradients = [
        (dot(left, right, 0, 0) + far.astype(F32)).astype(BF16)
        for left, right, far in zip(
            (acts[:, :width], acts[:, :width], h), (g, u, cots[:, :width]), sent
        )
    ]
    other, gradients = lax.optimization_barrier((other, gradients))
    return (plus(mine[0], other[:tokens]), plus(mine[2], other[tokens:]), *gradients)


def solution(mesh):
    return jax.shard_map(
        per_device,
        mesh=mesh,
        in_specs=(
            P("col", "row"),
            P("row", "col"),
            P("row", "col"),
            P("col", "row"),
            P("col", "row"),
        ),
        out_specs=(
            P("col", "row"),
            P("col", "row"),
            P("row", "col"),
            P("row", "col"),
            P("col", "row"),
        ),
        check_vma=False,
    )
```

```python
import jax
import jax.numpy as jnp
from jax import lax
from jax.experimental import pallas as pl
from jax.experimental.pallas import tpu as pltpu
from jax.sharding import PartitionSpec as P

BF16 = jnp.bfloat16
F32 = jnp.float32


def row_index(x, y, core):
    return (x * 4 + y) * 2 + core


def to_core(value):
    return lax.ppermute(value, "row", [(i, i ^ 1) for i in range(16)])


def row_shift(value, dx, dy):
    pairs = [
        (row_index(x, y, core), row_index(x ^ dx, (y + dy) % 4, core))
        for x in range(2)
        for y in range(4)
        for core in range(2)
    ]
    return lax.ppermute(value, "row", pairs)


def z_ring(value, ways):
    pairs = [
        (i * 16 + j, i * 16 + (j // 8) * 8 + (j % 8 + ways[i % 2]) % 8)
        for i in range(16)
        for j in range(16)
    ]
    return lax.ppermute(value, ("row", "col"), pairs)


def x_swap(value):
    return lax.ppermute(value, "col", [(j, j ^ 8) for j in range(16)])


def dot(left, right, left_dim, right_dim):
    return lax.dot_general(
        left, right, (((left_dim,), (right_dim,)), ((), ())), preferred_element_type=F32
    )


def swish_parts(gate):
    sigma = jax.nn.sigmoid(gate)
    return (gate * sigma, sigma * (1.0 + gate * (1.0 - sigma)))


def plus(left, right):
    return (left.astype(F32) + right.astype(F32)).astype(BF16)


def rows(parts):
    return jnp.concatenate(parts, axis=0)


def columns(parts):
    return jnp.concatenate(parts, axis=1)


def add_rows(value, start, more):
    stop = start + more.shape[0]
    parts = [value[:start], plus(value[start:stop], more), value[stop:]]
    return rows([part for part in parts if part.shape[0]])


def slot_numbers():
    row = lax.axis_index("row")
    core, y, x = row & 1, (row >> 1) & 3, row >> 3
    return core, core == 0, [(((p >> 1) - y) & 3) * 2 + ((p & 1) ^ x) for p in range(8)]


def unit_of(pair, which):
    size, width = pair.shape[0] // 2, pair.shape[1]
    return lax.dynamic_slice(
        pair.reshape(2, size, width), (which, 0, 0), (1, size, width), allow_negative_indices=False
    ).reshape(size, width)


def gather_col(pair, core, slots):
    size, width = pair.shape[0] // 2, pair.shape[1]
    units, block = [unit_of(pair, core)], pair
    for _ in range(3):
        block = z_ring(block, (1, -1))
        units += [block[:size], block[size:]]
    units.append(z_ring(unit_of(block, core), (1, -1)))
    total = jnp.zeros((8, size, width), BF16)
    for unit, slot in zip(units, slots):
        total = lax.dynamic_update_slice(
            total, unit.reshape(1, size, width), (slot, 0, 0), allow_negative_indices=False
        )
    return total.reshape(8 * size, width)


def scatter_y_x(parts):
    own, first, up, down, last = parts
    size = up.shape[0]
    up, down = row_shift(up, 0, 1), row_shift(down, 0, -1)
    up = row_shift(add_rows(first, 0, up), 0, 1)
    down = row_shift(add_rows(last, size, down), 0, -1)
    total = own.astype(F32) + up.astype(F32) + down.astype(F32)
    return total[:size] + row_shift(total[size:].astype(BF16), 1, 0).astype(F32)


def scatter_x_y(near, far):
    size = near.shape[0] // 4
    near = plus(near, row_shift(far, 1, 0))
    total = near[:size].astype(F32)
    for dy in (2, 1, 3):
        total = total + row_shift(near[dy * size : (dy + 1) * size], 0, dy).astype(F32)
    return total


def gather_row(share, other):
    size = share.shape[0]
    pair = rows([share, row_shift(share, 1, 0)])
    near = [other] + [row_shift(other, 0, -dy) for dy in (1, 2, 3)]
    last, first = row_shift(pair, 0, 1), row_shift(pair, 0, -1)
    near = rows(near)
    far = row_shift(near, 1, 0)
    up, down = row_shift(last[:size], 0, 1), row_shift(first[size:], 0, -1)
    return (pair, first, up, down, last), (near, far)


def scatter_units(partial, slots):
    size, width = partial.shape[0] // 8, partial.shape[1]
    return [
        lax.dynamic_slice(
            partial.reshape(8, size, width), (slot, 0, 0), (1, size, width), allow_negative_indices=False
        ).reshape(size, width)
        for slot in slots
    ]


def one_unit(unit, first):
    none = jnp.zeros_like(unit)
    return rows([jnp.where(first, unit, none), jnp.where(first, none, unit)])


def params(mib):
    return pltpu.CompilerParams(vmem_limit_bytes=mib * 2**20)


def whole_block(array):
    return pl.BlockSpec(array.shape, lambda step: (0, 0), pipeline_mode=pl.Buffered(1))


def gate_up_body(acts, gate, gate_other, up, up_other, *parts):
    width, units = gate.shape
    acts, acts_other = acts[:, :width], acts[:, width:]

    def store(columns_of, own, other):
        term = (dot(acts, own[...], 1, 0) + dot(acts_other, other[...], 1, 0)).astype(BF16)

        def put(parts):
            start = 0
            for part in parts:
                stop = start + part.shape[0]
                part[:, columns_of] = term[start:stop]
                start = stop

        @pl.when(pl.program_id(0) == 0)
        def _():
            put(parts[:2])

        @pl.when(pl.program_id(0) == 1)
        def _():
            put(parts[2:])

    store(slice(0, units), gate, gate_other)
    store(slice(units, 2 * units), up, up_other)


def gate_up_product(acts, weights):
    units = weights[0].shape[1]
    size = acts.shape[0] // 8
    shapes = [(n * size, 2 * units) for n in (2, 2, 1, 1, 2)]
    return pl.pallas_call(
        gate_up_body,
        grid=(2,),
        in_specs=[pl.BlockSpec((4 * size, acts.shape[1]), lambda n: (n, 0))]
        + [whole_block(weight) for weight in weights],
        out_specs=[pl.BlockSpec(shape, lambda n: (0, 0)) for shape in shapes],
        out_shape=[jax.ShapeDtypeStruct(shape, BF16) for shape in shapes],
        compiler_params=params(20),
    )(acts, *weights)


def hidden_grad_body(cots, down, down_other, near, far):
    width = down.shape[1]
    term = dot(cots[:, :width], down[...], 1, 1) + dot(cots[:, width:], down_other[...], 1, 1)
    term = term.astype(BF16)
    size = term.shape[0] // 4
    for n in range(2):
        near[n * size : (n + 1) * size, :] = term[2 * n * size : (2 * n + 1) * size]
        far[n * size : (n + 1) * size, :] = term[(2 * n + 1) * size : (2 * n + 2) * size]


def hidden_grad_product(cots, weights):
    units = weights[0].shape[0]
    size = cots.shape[0] // 8
    return pl.pallas_call(
        hidden_grad_body,
        grid=(2,),
        in_specs=[pl.BlockSpec((4 * size, cots.shape[1]), lambda n: (n, 0))]
        + [whole_block(weight) for weight in weights],
        out_specs=[pl.BlockSpec((2 * size, units), lambda n: (n, 0))] * 2,
        out_shape=[jax.ShapeDtypeStruct((4 * size, units), BF16)] * 2,
        compiler_params=params(16),
    )(cots, *weights)


def out_body(near, far, down, down_other, out, hidden):
    size = near.shape[0] // 2
    width = down.shape[1]
    for n in range(2):
        hidden[2 * n * size : (2 * n + 1) * size, :] = near[n * size : (n + 1) * size, :]
        hidden[(2 * n + 1) * size : (2 * n + 2) * size, :] = far[n * size : (n + 1) * size, :]
    out[:, :width] = dot(hidden[...], down[...], 1, 0).astype(BF16)
    out[:, width:] = dot(hidden[...], down_other[...], 1, 0).astype(BF16)


def halved(shape):
    return pl.BlockSpec((shape[0] // 2, shape[1]), lambda n: (n, 0))


def out_product(near, far, weights):
    units, width = weights[0].shape
    tokens = 2 * near.shape[0]
    shapes = [(tokens, 2 * width), (tokens, units)]
    return pl.pallas_call(
        out_body,
        grid=(2,),
        in_specs=[halved(near.shape)] * 2 + [whole_block(weight) for weight in weights],
        out_specs=[halved(shape) for shape in shapes],
        out_shape=[jax.ShapeDtypeStruct(shape, BF16) for shape in shapes],
        compiler_params=params(16),
    )(near, far, *weights)


def inner_body(
    g0, g1, g2, g3, g4, gate, gate_other, up, up_other, inner, gate_grad, up_grad
):
    width, units = gate.shape

    def assemble(parts):
        start = 0
        for part in parts:
            stop = start + part.shape[0]
            gate_grad[start:stop, :] = part[:, :units]
            up_grad[start:stop, :] = part[:, units:]
            start = stop

    @pl.when(pl.program_id(0) == 0)
    def _():
        assemble((g0, g1))

    @pl.when(pl.program_id(0) == 1)
    def _():
        assemble((g2, g3, g4))

    for n, (g, u) in enumerate(((gate, up), (gate_other, up_other))):
        inner[:, n * width : (n + 1) * width] = (
            dot(gate_grad[...], g[...], 1, 1) + dot(up_grad[...], u[...], 1, 1)
        ).astype(BF16)


def inner_product(grads, weights):
    width, units = weights[0].shape
    tokens = sum(part.shape[0] for part in grads)
    shapes = [(tokens, 2 * width)] + [(tokens, units)] * 2
    return pl.pallas_call(
        inner_body,
        grid=(2,),
        in_specs=[whole_block(array) for array in (*grads, *weights)],
        out_specs=[halved(shape) for shape in shapes],
        out_shape=[jax.ShapeDtypeStruct(shape, BF16) for shape in shapes],
        compiler_params=params(20),
    )(*grads, *weights)


def beside_body(own, other, pair):
    width = own.shape[1]
    pair[:, :width] = own[...]
    pair[:, width:] = other[...]


def with_partners(value):
    own = rows([value, x_swap(value)])
    return pl.pallas_call(
        beside_body,
        out_shape=jax.ShapeDtypeStruct((own.shape[0], 2 * own.shape[1]), BF16),
        compiler_params=params(8),
    )(own, to_core(own))


def per_device(activations, weight_gate, weight_up, weight_down, out_cotangent):
    width, units = weight_gate.shape
    tokens = activations.shape[0]
    (core, first, slots), activations, out_cotangent = lax.optimization_barrier(
        (slot_numbers(), activations, out_cotangent)
    )

    acts, cots = with_partners(activations), with_partners(out_cotangent)
    weights = (weight_gate, weight_up, weight_down)
    gate_weights, up_weights, down_weights = ((w, to_core(w)) for w in weights)
    acts, cots = gather_col(acts, core, slots), gather_col(cots, core, slots)
    hidden_grad = scatter_x_y(*hidden_grad_product(cots, down_weights))
    gate_up = scatter_y_x(gate_up_product(acts, (*gate_weights, *up_weights)))
    gate, up_value = gate_up[:, :units], gate_up[:, units:]
    swish, slope = swish_parts(gate)
    grad_share = columns(
        [
            (hidden_grad * up_value * slope).astype(BF16),
            (hidden_grad * swish).astype(BF16),
        ]
    )
    hidden_share = (swish * up_value).astype(BF16)
    grads, (near, far) = gather_row(grad_share, hidden_share)
    block_out, hidden = out_product(near, far, down_weights)
    input_gradient, gate_grad, up_grad = inner_product(grads, (*gate_weights, *up_weights))

    partials = [scatter_units(partial, slots) for partial in (block_out, input_gradient)]
    sums = [z_ring(units[7], (-1, 1)) for units in partials]
    (h, g, u), sums[1] = lax.optimization_barrier(((hidden, gate_grad, up_grad), sums[1]))
    sent = [
        to_core(dot(left, right, 0, 0).astype(BF16))
        for left, right in ((acts[:, width:], g), (acts[:, width:], u), (h, cots[:, width:]))
    ]
    sums = [one_unit(total, first) for total in sums]
    for p in (5, 3, 1):
        sums = [
            z_ring(plus(rows(units[p : p + 2]), total), (-1, 1))
            for units, total in zip(partials, sums)
        ]
    total = rows(
        [plus(one_unit(units[0], first), total) for units, total in zip(partials, sums)]
    )
    total = plus(total[:, :width], to_core(total[:, width:]))
    total, sent = lax.optimization_barrier((total, sent))
    mine = [total[n * tokens : (n + 1) * tokens] for n in range(4)]
    other = x_swap(rows([mine[1], mine[3]]))
    gradients = [
        (dot(left, right, 0, 0) + far.astype(F32)).astype(BF16)
        for left, right, far in zip(
            (acts[:, :width], acts[:, :width], h), (g, u, cots[:, :width]), sent
        )
    ]
    other, gradients = lax.optimization_barrier((other, gradients))
    return (plus(mine[0], other[:tokens]), plus(mine[2], other[tokens:]), *gradients)


def solution(mesh):
    return jax.shard_map(
        per_device,
        mesh=mesh,
        in_specs=(
            P("col", "row"),
            P("row", "col"),
            P("row", "col"),
            P("col", "row"),
            P("col", "row"),
        ),
        out_specs=(
            P("col", "row"),
            P("col", "row"),
            P("row", "col"),
            P("row", "col"),
            P("col", "row"),
        ),
        check_vma=False,
    )
```
